32 devices in a mesh: dp: 2 (over x), outer: 8 (over z, core), inner: 2 (over y).
Axes of the slice: x: 2, y: 2, z: 4, core: 2. Of those that a mesh axis runs over, the one named last changes fastest.
Arguments:
- queries: bfloat16 [2048, 4096], P(('outer', 'inner'), 'dp'), may hold values from -512 to 512
- out_grad: bfloat16 [2048, 4096], P(('outer', 'inner'), 'dp'), may hold values from -6 to 6
- key_rows: bfloat16 [2048, 512], P(('outer', 'inner')), may hold values from -14 to 14
- value_rows: bfloat16 [2048, 512], P(('outer', 'inner')), may hold values from -6 to 6
- block_order: int32 [16], replicated, may hold values from 0 to 15, each once
- block_flags: int32 [16, 3], replicated, may hold values 0 or 1
Outputs:
- query_grad: bfloat16 [2048, 4096], P(('outer', 'inner'), 'dp')
- key_grad: float32 [2048, 512], P(('outer', 'inner'), 'dp')
- value_grad: float32 [2048, 512], P(('outer', 'inner'), 'dp')
The draws below stay inside these ranges and needn't reach their ends.
Inputs may be any that keep to these rules, and one draw needn't show every extreme that they name: `block_order`: each number appears once.
All inputs are finite; a program needn't handle non-finite values.
Results may differ from the reference program's by a relative error of at most 0.005.
Values may be sent and summed in bfloat16 or wider, within the bound.
A program may use at most 64 MiB of HBM per device.

```python
import math
import jax
import jax.numpy as jnp
from jax import lax

HEADS = 32
KV_HEADS = 4
HD = 128
ROWS = 128
SHARDS = 16
SLOTS = 3
TOKENS = 2048
N_OUTER = 8
N_INNER = 2


def shared_keys(key):
    base_draw = jnp.clip(jax.random.normal(jax.random.fold_in(key, 7), (TOKENS, KV_HEADS, HD), jnp.float32), -4.5, 4.5)
    return base_draw


def draw_key_rows(key, part):
    key_draw = shared_keys(key)
    return key_draw.reshape(TOKENS, KV_HEADS * HD).astype(jnp.bfloat16)


def draw_queries(key, part):
    raw_draw = jnp.clip(jax.random.normal(jax.random.fold_in(key, 11), (TOKENS, HEADS // KV_HEADS, KV_HEADS, HD), jnp.float32), -4.5, 4.5)
    return raw_draw.reshape(TOKENS, HEADS * HD).astype(jnp.bfloat16)


def touch_ends(entries, stream_key, smallest, high):
    spot = [jax.random.randint(jax.random.fold_in(stream_key, axis), (), 0, length) for axis, length in enumerate(entries.shape)]
    longest = entries.shape.index(max(entries.shape))
    beside = spot[:longest] + [(spot[longest] + 1) % entries.shape[longest]] + spot[longest + 1:]
    return entries.at[tuple(spot)].set(smallest).at[tuple(beside)].set(high)


def block_levels(key, shape, pieces, smallest, top_value):
    loudness, own = 1.0, jax.random.fold_in(key, 6)
    for axis_at, shards_of in pieces:
        steps = jnp.exp(jax.random.uniform(jax.random.fold_in(own, axis_at), (shards_of,), jnp.float32, smallest / len(pieces), top_value / len(pieces)))
        loudness = loudness * jnp.repeat(steps, shape[axis_at] // shards_of).reshape([-1 if axis == axis_at else 1 for axis in range(len(shape))])
    return loudness


def gaussian(stream_key, shape, spread, bound, pieces=(), held_as=jnp.bfloat16):
    entries = jax.random.normal(stream_key, shape, jnp.float32) * spread
    if len(pieces) > 0:
        entries = block_levels(stream_key, shape, pieces, -0.22, 0.18) * entries
    return jnp.clip(entries, min=-bound, max=bound).astype(held_as)


def setup_inputs(seed: int = 0) -> dict:
    key_of = jax.random.split(jax.random.key(seed), 7)
    return {
        "queries": draw_queries(jax.random.fold_in(key_of[6], 71), 0),
        "out_grad": gaussian(key_of[1], (TOKENS, HEADS * HD), 1.0, 6.0, ((0, 16), (1, 2))),
        "key_rows": draw_key_rows(jax.random.fold_in(key_of[6], 71), 0),
        "value_rows": gaussian(key_of[3], (TOKENS, KV_HEADS * HD), 1.0, 6.0, ((0, 16),)),
        "block_order": jax.random.permutation(key_of[4], SHARDS).astype(jnp.int32),
        "block_flags": touch_ends((jax.random.randint(key_of[5], (SHARDS, SLOTS), 0, 4) < 3).astype(jnp.int32), jax.random.fold_in(key_of[5], 1), 0, 1),
    }


def window_grads(query_block, grad_block, key_window, value_window, visible, score_scale):
    query_wide = query_block.astype(jnp.float32)
    grad_wide = grad_block.astype(jnp.float32)
    key_wide = key_window.astype(jnp.float32)
    value_wide = value_window.astype(jnp.float32)
    seen = visible[:, None, None, :]
    scores = jnp.einsum('rgjd,wjd->rgjw', query_wide, key_wide) * score_scale
    row_max = lax.optimization_barrier(jnp.max(jnp.where(seen, scores, -jnp.inf), axis=-1, keepdims=True))
    exp_scores = jnp.where(seen, jnp.exp(scores - row_max), 0.0)
    soft_weights = exp_scores / lax.optimization_barrier(jnp.sum(exp_scores, axis=-1, keepdims=True))
    soft_low = lax.optimization_barrier(soft_weights.astype(jnp.bfloat16)).astype(jnp.float32)
    weight_grads = jnp.einsum('rgjd,wjd->rgjw', grad_wide, value_wide)
    row_delta = lax.optimization_barrier(jnp.sum(soft_weights * weight_grads, axis=-1, keepdims=True))
    score_grads = (soft_weights * (weight_grads - row_delta) * score_scale).astype(jnp.bfloat16)
    score_wide = lax.optimization_barrier(score_grads).astype(jnp.float32)
    query_part = jnp.einsum('rgjw,wjd->rgjd', score_wide, key_wide).astype(jnp.bfloat16)
    key_part = jnp.einsum('rgjw,rgjd->wjd', score_wide, query_wide)
    value_part = jnp.einsum('rgjw,rgjd->wjd', soft_low, grad_wide)
    return (query_part, key_part, value_part)

def reference(queries, out_grad, key_rows, value_rows, block_order, block_flags):
    score_scale = 1.0 / math.sqrt(HD)
    group_count = HEADS // KV_HEADS
    shard_total = N_OUTER * N_INNER
    query_shards = queries.reshape(shard_total, ROWS, group_count, KV_HEADS, HD)
    grad_shards = out_grad.reshape(shard_total, ROWS, group_count, KV_HEADS, HD)
    key_table = key_rows.reshape(TOKENS, KV_HEADS, HD)
    value_table = value_rows.reshape(TOKENS, KV_HEADS, HD)
    row_index = jnp.arange(ROWS, dtype=jnp.int32)
    positions = (block_order[:, None] * ROWS + row_index[None, :]).astype(jnp.int32)
    slot_index = jnp.arange(N_INNER + 1, dtype=jnp.int32)
    group_span = N_INNER * ROWS

    def step(totals, shard_index):
        key_total, value_total = totals
        outer_index = shard_index // N_INNER
        member_index = shard_index % N_INNER
        previous = (outer_index + N_OUTER - 1) % N_OUTER * N_INNER + member_index
        group_start = (outer_index * group_span).astype(jnp.int32)
        prev_start = (previous * ROWS).astype(jnp.int32)
        key_window = jnp.concatenate([lax.dynamic_slice_in_dim(key_table, group_start, group_span, 0), lax.dynamic_slice_in_dim(key_table, prev_start, ROWS, 0)], 0)
        value_window = jnp.concatenate([lax.dynamic_slice_in_dim(value_table, group_start, group_span, 0), lax.dynamic_slice_in_dim(value_table, prev_start, ROWS, 0)], 0)
        group_pos = lax.dynamic_slice_in_dim(positions, (outer_index * N_INNER).astype(jnp.int32), N_INNER, 0).reshape(-1)
        key_pos = jnp.concatenate([group_pos, positions[previous]], 0)
        allowed = (block_flags[shard_index] == 1) | (slot_index == member_index)
        visible = (key_pos[None, :] <= positions[shard_index][:, None]) & jnp.repeat(allowed, ROWS)[None, :]
        query_part, key_part, value_part = window_grads(query_shards[shard_index], grad_shards[shard_index], key_window, value_window, visible, score_scale)
        key_total = lax.dynamic_update_slice_in_dim(key_total, lax.dynamic_slice_in_dim(key_total, group_start, group_span, 0) + key_part[:group_span], group_start, 0)
        key_total = lax.dynamic_update_slice_in_dim(key_total, lax.dynamic_slice_in_dim(key_total, prev_start, ROWS, 0) + key_part[group_span:], prev_start, 0)
        value_total = lax.dynamic_update_slice_in_dim(value_total, lax.dynamic_slice_in_dim(value_total, group_start, group_span, 0) + value_part[:group_span], group_start, 0)
        value_total = lax.dynamic_update_slice_in_dim(value_total, lax.dynamic_slice_in_dim(value_total, prev_start, ROWS, 0) + value_part[group_span:], prev_start, 0)
        return ((key_total, value_total), query_part)
    zero_sums = jnp.zeros((TOKENS, KV_HEADS, HD), jnp.float32)
    (key_total, value_total), query_parts = lax.scan(step, (zero_sums, zero_sums), jnp.arange(shard_total, dtype=jnp.int32))
    return (query_parts.reshape(TOKENS, HEADS * HD), key_total.reshape(TOKENS, KV_HEADS * HD), value_total.reshape(TOKENS, KV_HEADS * HD))
```

```python
import functools
import math

import jax
import jax.numpy as jnp
from jax import lax
from jax.experimental import pallas as pl
from jax.experimental.pallas import tpu as pltpu
from jax.sharding import PartitionSpec as P

HD = 128
HIDDEN = -1e30
MESH = pl.DeviceIdType.MESH


def kernel(
    sizes,
    q_hbm,
    g_hbm,
    k_hbm,
    v_hbm,
    order,
    flags,
    qg_out,
    kg_out,
    vg_out,
    q,
    g,
    kw,
    vw,
    acc,
    grad_out,
    grad_in,
    half_out,
    half_in,
    local_sem,
    kv_send,
    kv_recv,
    grad_send,
    grad_recv,
    half_send,
    half_recv,
):
    n_dp, n_outer, n_inner, heads, groups = sizes
    rows = q.shape[0]
    slots = n_inner + 1
    mine = heads // n_dp
    dp, outer, inner = (lax.axis_index(name) for name in ("dp", "outer", "inner"))
    lower = lax.rem(outer + n_outer - 1, n_outer)
    upper = lax.rem(outer + 1, n_outer)

    def owner(slot):
        return {"outer": lower} if slot == n_inner else {"inner": lax.rem(inner + slot, n_inner)}

    def reader(slot):
        if slot == n_inner:
            return {"outer": upper}
        return {"inner": lax.rem(inner + n_inner - slot, n_inner)}

    def columns(head):
        return pl.ds(pl.multiple_of(head * HD, HD), HD)

    step_heads = [lax.rem(mine * (dp + 1) + k, heads) for k in range(heads)]

    local = [
        pltpu.make_async_copy(src, dst, local_sem.at[i])
        for i, (src, dst) in enumerate(
            ((k_hbm, kw.at[pl.ds(0, rows)]), (q_hbm, q), (v_hbm, vw.at[pl.ds(0, rows)]), (g_hbm, g))
        )
    ]
    for copy in local:
        copy.start()

    barrier = pltpu.get_barrier_semaphore()
    near = [{"inner": lax.rem(inner + i, n_inner)} for i in range(1, n_inner)]
    near += [{"dp": lax.rem(dp + i, n_dp)} for i in range(1, n_dp)]
    near += [{"outer": lower}, {"outer": upper}]
    for device in near:
        pl.semaphore_signal(barrier, inc=1, device_id=device, device_id_type=MESH)
    pl.semaphore_wait(barrier, len(near))

    arrivals = []
    for k in range(heads):
        cols = columns(step_heads[k])
        for slot in range(1, slots):
            for which, (src, dst) in enumerate(((k_hbm, kw), (v_hbm, vw))):
                copy = pltpu.make_async_remote_copy(
                    src_ref=src.at[:, cols],
                    dst_ref=dst.at[pl.ds(slot * rows, rows), cols],
                    send_sem=kv_send.at[k, slot - 1, which],
                    recv_sem=kv_recv.at[k, slot - 1, which],
                    device_id=reader(slot),
                    device_id_type=MESH,
                )
                copy.start()
                arrivals.append((k, copy))

    shard = outer * n_inner + inner
    own_block = order[shard]
    bias = []
    for slot in range(1, slots):
        if slot == n_inner:
            place, block = n_inner, order[lower * n_inner + inner]
        else:
            place = lax.rem(inner + slot, n_inner)
            block = order[outer * n_inner + place]
        seen = (flags[shard, place] == 1) & (block < own_block)
        bias.append(jnp.where(seen, 0.0, HIDDEN).astype(jnp.float32))

    wide = groups * rows
    key_at = lax.broadcasted_iota(jnp.int32, (rows, wide), 0)
    query_at = lax.rem(lax.broadcasted_iota(jnp.int32, (rows, wide), 1), rows)
    causal = key_at <= query_at
    scale = 1.0 / math.sqrt(HD)
    to_exp2 = scale * math.log2(math.e)

    def nt(a, b):
        return lax.dot_general(a, b, (((1,), (1,)), ((), ())), preferred_element_type=jnp.float32)

    def nn(a, b):
        return jnp.dot(a, b, preferred_element_type=jnp.float32)

    grads = []
    halves = []

    def settle(k):
        for slot in range(1, slots):
            grads[k * (slots - 1) + slot - 1].wait_recv()
        total = acc[k]
        for slot in range(1, slots):
            total += grad_in[k, slot - 1].astype(jnp.float32)
        if k < heads - mine:
            half_out[k] = total.astype(jnp.bfloat16)
            copy = pltpu.make_async_remote_copy(
                src_ref=half_out.at[k],
                dst_ref=half_in.at[k],
                send_sem=half_send.at[k],
                recv_sem=half_recv.at[k],
                device_id={"dp": lax.rem(dp + 1 + k // mine, n_dp)},
                device_id_type=MESH,
            )
            copy.start()
            halves.append(copy)
        else:
            at = k - (heads - mine)
            for d in range(n_dp - 1):
                halves[d * mine + at].wait_recv()
                total += half_in[d * mine + at].astype(jnp.float32)
            kg_out[:, at * HD : (at + 1) * HD] = total[0]
            vg_out[:, at * HD : (at + 1) * HD] = total[1]

    for copy in local:
        copy.wait()
    for k in range(heads):
        head = step_heads[k]
        cols = columns(head)
        group_cols = [columns(n * heads + head) for n in range(groups)]
        q_all = jnp.concatenate([q[:, c] for c in group_cols], 0)
        g_all = jnp.concatenate([g[:, c] for c in group_cols], 0)
        for step, copy in arrivals:
            if step == k:
                copy.wait_recv()
        keys = kw[:, cols]
        values = vw[:, cols]
        scores = nt(keys, q_all)
        weight_grads = nt(values, g_all)
        parts = [scores[c * rows : (c + 1) * rows] for c in range(slots)]
        parts[0] = jnp.where(causal, parts[0], HIDDEN)
        tops = [jnp.max(part, 0, keepdims=True) for part in parts]
        top = tops[0]
        for c in range(1, slots):
            top = jnp.maximum(top, tops[c] + bias[c - 1])
        exps = [
            jnp.exp2((part - (top if c == 0 else top - bias[c - 1])) * to_exp2)
            for c, part in enumerate(parts)
        ]
        weights = jnp.concatenate(exps, 0)
        soft = weights * (1.0 / jnp.sum(weights, 0, keepdims=True))
        delta = jnp.sum(soft * weight_grads, 0, keepdims=True)
        score_grads = (soft * (weight_grads - delta) * scale).astype(jnp.bfloat16)
        soft_low = soft.astype(jnp.bfloat16)
        key_part = nn(score_grads, q_all)
        value_part = nn(soft_low, g_all)
        acc[k, 0] = key_part[:rows]
        acc[k, 1] = value_part[:rows]
        for slot in range(1, slots):
            grad_out[k, slot - 1, 0] = key_part[slot * rows : (slot + 1) * rows].astype(jnp.bfloat16)
            grad_out[k, slot - 1, 1] = value_part[slot * rows : (slot + 1) * rows].astype(jnp.bfloat16)
            copy = pltpu.make_async_remote_copy(
                src_ref=grad_out.at[k, slot - 1],
                dst_ref=grad_in.at[k, slot - 1],
                send_sem=grad_send.at[k, slot - 1],
                recv_sem=grad_recv.at[k, slot - 1],
                device_id=owner(slot),
                device_id_type=MESH,
            )
            copy.start()
            grads.append(copy)
        query_part = nn(keys.T, score_grads)
        for n in range(groups):
            qg_out[:, group_cols[n]] = query_part[:, n * rows : (n + 1) * rows].T.astype(jnp.bfloat16)
        if k >= 2:
            settle(k - 2)
    for k in range(max(heads - 2, 0), heads):
        settle(k)
    for _, copy in arrivals:
        copy.wait_send()
    for copy in grads + halves:
        copy.wait_send()


def solution(mesh):
    n_dp, n_outer, n_inner = (mesh.shape[name] for name in ("dp", "outer", "inner"))

    def body(queries, out_grad, key_rows, value_rows, block_order, block_flags):
        rows, width = queries.shape
        heads = key_rows.shape[1] // HD
        groups = width // (heads * HD)
        mine = heads // n_dp
        others = n_inner
        bf16, f32 = jnp.bfloat16, jnp.float32
        window = (n_inner + 1) * rows
        any_space = pl.BlockSpec(memory_space=pl.ANY)
        smem = pl.BlockSpec(memory_space=pltpu.SMEM)
        vmem = pl.BlockSpec(memory_space=pltpu.VMEM)
        dma = pltpu.SemaphoreType.DMA
        return pl.pallas_call(
            functools.partial(kernel, (n_dp, n_outer, n_inner, heads, groups)),
            out_shape=(
                jax.ShapeDtypeStruct((rows, width), bf16),
                jax.ShapeDtypeStruct((rows, mine * HD), f32),
                jax.ShapeDtypeStruct((rows, mine * HD), f32),
            ),
            in_specs=[any_space] * 4 + [smem] * 2,
            out_specs=(vmem, vmem, vmem),
            scratch_shapes=[
                pltpu.VMEM((rows, width), bf16),
                pltpu.VMEM((rows, width), bf16),
                pltpu.VMEM((window, heads * HD), bf16),
                pltpu.VMEM((window, heads * HD), bf16),
                pltpu.VMEM((heads, 2, rows, HD), f32),
                pltpu.VMEM((heads, others, 2, rows, HD), bf16),
                pltpu.VMEM((heads, others, 2, rows, HD), bf16),
                pltpu.VMEM((heads - mine, 2, rows, HD), bf16),
                pltpu.VMEM((heads - mine, 2, rows, HD), bf16),
                dma((4,)),
                dma((heads, others, 2)),
                dma((heads, others, 2)),
                dma((heads, others)),
                dma((heads, others)),
                dma((heads - mine,)),
                dma((heads - mine,)),
            ],
            compiler_params=pltpu.CompilerParams(
                collective_id=0, has_side_effects=True, vmem_limit_bytes=40 * 1024 * 1024
            ),
        )(queries, out_grad, key_rows, value_rows, block_order, block_flags)

    spread = P(("outer", "inner"), "dp")
    return jax.shard_map(
        body,
        mesh=mesh,
        in_specs=(spread, spread, P(("outer", "inner"), None), P(("outer", "inner"), None), P(), P()),
        out_specs=(spread, spread, spread),
        check_vma=False,
    )
```

```python
import functools
import math

import jax
import jax.numpy as jnp
from jax import lax
from jax.experimental import pallas as pl
from jax.experimental.pallas import tpu as pltpu
from jax.sharding import PartitionSpec as P

HD = 128
HIDDEN = -1e30
MESH = pl.DeviceIdType.MESH


def kernel(
    sizes,
    q_hbm,
    g_hbm,
    k_hbm,
    v_hbm,
    order,
    flags,
    qg_out,
    kg_out,
    vg_out,
    q,
    g,
    kw,
    vw,
    acc,
    grad_out,
    grad_in,
    half_out,
    half_in,
    local_sem,
    kv_send,
    kv_recv,
    grad_send,
    grad_recv,
    half_send,
    half_recv,
    cross_in,
    cross_recv,
    pass_send,
):
    n_dp, n_outer, n_inner, heads, groups = sizes
    rows = q.shape[0]
    slots = n_inner + 1
    mine = heads // n_dp
    dp, outer, inner = (lax.axis_index(name) for name in ("dp", "outer", "inner"))
    lower = lax.rem(outer + n_outer - 1, n_outer)
    upper = lax.rem(outer + 1, n_outer)

    def owner(slot):
        return {"outer": lower} if slot == n_inner else {"inner": lax.rem(inner + slot, n_inner)}

    def reader(slot):
        if slot == n_inner:
            return {"outer": upper}
        return {"inner": lax.rem(inner + n_inner - slot, n_inner)}

    def columns(head):
        return pl.ds(pl.multiple_of(head * HD, HD), HD)

    step_heads = [lax.rem(mine * (dp + 1) + k, heads) for k in range(heads)]

    local = [
        pltpu.make_async_copy(src, dst, local_sem.at[i])
        for i, (src, dst) in enumerate(
            ((k_hbm, kw.at[pl.ds(0, rows)]), (q_hbm, q), (v_hbm, vw.at[pl.ds(0, rows)]), (g_hbm, g))
        )
    ]
    for copy in local:
        copy.start()

    barrier = pltpu.get_barrier_semaphore()
    near = [{"inner": lax.rem(inner + i, n_inner)} for i in range(1, n_inner)]
    near += [{"dp": lax.rem(dp + i, n_dp)} for i in range(1, n_dp)]
    near += [{"outer": lower}, {"outer": upper}]
    for device in near:
        pl.semaphore_signal(barrier, inc=1, device_id=device, device_id_type=MESH)
    pl.semaphore_wait(barrier, len(near))

    def window(ref, slot, k):
        return ref.at[pl.ds(slot * rows, rows), columns(step_heads[k])]

    def arriving(src, dst, k, slot, which, send_sem, device, at):
        return pltpu.make_async_remote_copy(
            src_ref=src,
            dst_ref=window(dst, slot, k),
            send_sem=send_sem,
            recv_sem=kv_recv.at[at, slot - 1, which],
            device_id=device,
            device_id_type=MESH,
        )

    pairs = ((k_hbm, kw), (v_hbm, vw))
    arrivals = {}
    sent = []
    for k in range(heads):
        for slot in range(1, slots):
            direct = slot == n_inner or k < mine
            for which, (src, dst) in enumerate(pairs):
                block = src.at[:, columns(step_heads[k])] if direct else window(dst, slot, k)
                copy = arriving(
                    block, dst, k, slot, which, kv_send.at[k, slot - 1, which], reader(slot), k
                )
                if direct:
                    copy.start()
                    sent.append(copy)
                arrivals[k, slot, which] = copy

    def arrive(k):
        for slot in range(1, slots):
            for which, (_, dst) in enumerate(pairs):
                arrivals[k, slot, which].wait_recv()
                if slot == n_inner or k >= mine:
                    continue
                for d in range(1, n_dp):
                    copy = arriving(
                        window(dst, slot, k),
                        dst,
                        k,
                        slot,
                        which,
                        pass_send.at[d - 1, k, slot - 1, which],
                        {"dp": lax.rem(dp + d, n_dp)},
                        mine * (n_dp - d) + k,
                    )
                    copy.start()
                    sent.append(copy)

    shard = outer * n_inner + inner
    own_block = order[shard]
    bias = []
    for slot in range(1, slots):
        if slot == n_inner:
            place, block = n_inner, order[lower * n_inner + inner]
        else:
            place = lax.rem(inner + slot, n_inner)
            block = order[outer * n_inner + place]
        seen = (flags[place, shard] == 1) & (block < own_block)
        bias.append(jnp.where(seen, 0.0, HIDDEN).astype(jnp.float32))

    wide = groups * rows
    key_at = lax.broadcasted_iota(jnp.int32, (rows, wide), 0)
    query_at = lax.rem(lax.broadcasted_iota(jnp.int32, (rows, wide), 1), rows)
    causal = key_at <= query_at
    scale = 1.0 / math.sqrt(HD)
    to_exp2 = scale * math.log2(math.e)

    def nt(a, b):
        return lax.dot_general(a, b, (((1,), (1,)), ((), ())), preferred_element_type=jnp.float32)

    def nn(a, b):
        return jnp.dot(a, b, preferred_element_type=jnp.float32)

    grads = {}
    crossing = {}
    halves = []

    def crosses(k, slot):
        return slot < n_inner and k < heads - mine and k % mine < mine // 2


    def settle(k):
        total = acc[k]
        for slot in range(1, slots):
            if crosses(k, slot):
                continue
            grads[k, slot].wait_recv()
            total += grad_in[k, slot - 1].astype(jnp.float32)
        if k < heads - mine:
            half_out[k] = total.astype(jnp.bfloat16)
            copy = pltpu.make_async_remote_copy(
                src_ref=half_out.at[k],
                dst_ref=half_in.at[k],
                send_sem=half_send.at[k],
                recv_sem=half_recv.at[k],
                device_id={"dp": lax.rem(dp + 1 + k // mine, n_dp)},
                device_id_type=MESH,
            )
            copy.start()
            halves.append(copy)
        else:
            at = k - (heads - mine)
            for d in range(n_dp - 1):
                halves[d * mine + at].wait_recv()
                total += half_in[d * mine + at].astype(jnp.float32)
            kg_out[:, at * HD : (at + 1) * HD] = total[0]
            vg_out[:, at * HD : (at + 1) * HD] = total[1]

    for copy in local:
        copy.wait()
    for k in range(heads):
        head = step_heads[k]
        cols = columns(head)
        group_cols = [columns(n * heads + head) for n in range(groups)]
        q_all = jnp.concatenate([q[:, c] for c in group_cols], 0)
        g_all = jnp.concatenate([g[:, c] for c in group_cols], 0)
        arrive(k)
        keys = kw[:, cols]
        values = vw[:, cols]
        scores = nt(keys, q_all)
        weight_grads = nt(values, g_all)
        parts = [scores[c * rows : (c + 1) * rows] for c in range(slots)]
        parts[0] = jnp.where(causal, parts[0], HIDDEN)
        tops = [jnp.max(part, 0, keepdims=True) for part in parts]
        top = tops[0]
        for c in range(1, slots):
            top = jnp.maximum(top, tops[c] + bias[c - 1])
        exps = [
            jnp.exp2((part - (top if c == 0 else top - bias[c - 1])) * to_exp2)
            for c, part in enumerate(parts)
        ]
        weights = jnp.concatenate(exps, 0)
        soft = weights * (1.0 / jnp.sum(weights, 0, keepdims=True))
        delta = jnp.sum(soft * weight_grads, 0, keepdims=True)
        score_grads = (soft * (weight_grads - delta) * scale).astype(jnp.bfloat16)
        soft_low = soft.astype(jnp.bfloat16)
        key_part = nn(score_grads, q_all)
        value_part = nn(soft_low, g_all)
        acc[k, 0] = key_part[:rows]
        acc[k, 1] = value_part[:rows]
        for slot in range(1, slots):
            terms = [x[slot * rows : (slot + 1) * rows] for x in (key_part, value_part)]
            at = k - (heads - mine)
            if at >= 0 and slot < n_inner and at < mine // 2:
                for d in range(n_dp - 1):
                    crossing[d * mine + at, slot].wait_recv()
                    for which in range(2):
                        terms[which] += cross_in[d * mine + at, slot - 1, which].astype(jnp.float32)
            for which in range(2):
                grad_out[k, slot - 1, which] = terms[which].astype(jnp.bfloat16)
            if crosses(k, slot):
                copy = pltpu.make_async_remote_copy(
                    src_ref=grad_out.at[k, slot - 1],
                    dst_ref=cross_in.at[k, slot - 1],
                    send_sem=grad_send.at[k, slot - 1],
                    recv_sem=cross_recv.at[k, slot - 1],
                    device_id={"dp": lax.rem(dp + 1 + k // mine, n_dp)},
                    device_id_type=MESH,
                )
                crossing[k, slot] = copy
            else:
                copy = pltpu.make_async_remote_copy(
                    src_ref=grad_out.at[k, slot - 1],
                    dst_ref=grad_in.at[k, slot - 1],
                    send_sem=grad_send.at[k, slot - 1],
                    recv_sem=grad_recv.at[k, slot - 1],
                    device_id=owner(slot),
                    device_id_type=MESH,
                )
                grads[k, slot] = copy
            copy.start()
        query_part = nn(keys.T, score_grads)
        for n in range(groups):
            qg_out[:, group_cols[n]] = query_part[:, n * rows : (n + 1) * rows].T.astype(jnp.bfloat16)
        if k >= 2:
            settle(k - 2)
    for k in range(max(heads - 2, 0), heads):
        settle(k)
    for copy in sent + list(grads.values()) + list(crossing.values()) + halves:
        copy.wait_send()


def place(*refs):
    *arrays, sems = refs
    copies = [
        pltpu.make_async_copy(arrays[i], arrays[i + 3], sems.at[i]) for i in range(3)
    ]
    for copy in copies:
        copy.start()
    for copy in copies:
        copy.wait()


def solution(mesh):
    n_dp, n_outer, n_inner = (mesh.shape[name] for name in ("dp", "outer", "inner"))

    def body(queries, out_grad, key_rows, value_rows, block_order, block_flags):
        rows, width = queries.shape
        heads = key_rows.shape[1] // HD
        groups = width // (heads * HD)
        mine = heads // n_dp
        others = n_inner
        bf16, f32 = jnp.bfloat16, jnp.float32
        window = (n_inner + 1) * rows
        any_space = pl.BlockSpec(memory_space=pl.ANY)
        smem = pl.BlockSpec(memory_space=pltpu.SMEM)
        vmem = pl.BlockSpec(memory_space=pltpu.VMEM)
        dma = pltpu.SemaphoreType.DMA
        operands = [
            pltpu.with_memory_space_constraint(x, pltpu.HBM)
            for x in (queries, out_grad, key_rows, value_rows, block_order, block_flags.T)
        ]
        results = pl.pallas_call(
            functools.partial(kernel, (n_dp, n_outer, n_inner, heads, groups)),
            out_shape=(
                pltpu.VMEM((rows, width), bf16),
                pltpu.VMEM((rows, mine * HD), f32),
                pltpu.VMEM((rows, mine * HD), f32),
            ),
            in_specs=[any_space] * 4 + [smem] * 2,
            out_specs=(vmem, vmem, vmem),
            scratch_shapes=[
                pltpu.VMEM((rows, width), bf16),
                pltpu.VMEM((rows, width), bf16),
                pltpu.VMEM((window, heads * HD), bf16),
                pltpu.VMEM((window, heads * HD), bf16),
                pltpu.VMEM((heads, 2, rows, HD), f32),
                pltpu.VMEM((heads, others, 2, rows, HD), bf16),
                pltpu.VMEM((heads, others, 2, rows, HD), bf16),
                pltpu.VMEM((heads - mine, 2, rows, HD), bf16),
                pltpu.VMEM((heads - mine, 2, rows, HD), bf16),
                dma((4,)),
                dma((heads, others, 2)),
                dma((heads, others, 2)),
                dma((heads, others)),
                dma((heads, others)),
                dma((heads - mine,)),
                dma((heads - mine,)),
                pltpu.VMEM((heads - mine, others, 2, rows, HD), bf16),
                dma((heads - mine, others)),
                dma((n_dp - 1, mine, others, 2)),
            ],
            compiler_params=pltpu.CompilerParams(
                collective_id=0, has_side_effects=True, vmem_limit_bytes=40 * 1024 * 1024
            ),
        )(*operands)
        return pl.pallas_call(
            place,
            out_shape=tuple(pltpu.HBM(x.shape, x.dtype) for x in results),
            in_specs=[vmem] * 3,
            out_specs=(any_space,) * 3,
            scratch_shapes=[dma((3,))],
        )(*(pltpu.with_memory_space_constraint(x, pltpu.VMEM) for x in results))

    spread = P(("outer", "inner"), "dp")
    return jax.shard_map(
        body,
        mesh=mesh,
        in_specs=(spread, spread, P(("outer", "inner"), None), P(("outer", "inner"), None), P(), P()),
        out_specs=(spread, spread, spread),
        check_vma=False,
    )
```

```python
import functools
import math

import jax
import jax.numpy as jnp
from jax import lax
from jax.experimental import pallas as pl
from jax.experimental.pallas import tpu as pltpu
from jax.sharding import PartitionSpec as P

HD = 128
HIDDEN = -1e30
MESH = pl.DeviceIdType.MESH


def kernel(
    sizes,
    q_hbm,
    g_hbm,
    k_hbm,
    v_hbm,
    order,
    flags,
    qg_out,
    kg_out,
    vg_out,
    q,
    g,
    kw,
    vw,
    acc,
    grad_out,
    grad_in,
    half_out,
    half_in,
    local_sem,
    kv_send,
    kv_recv,
    grad_send,
    grad_recv,
    half_send,
    half_recv,
    cross_in,
    cross_recv,
    pass_send,
    own,
):
    n_dp, n_outer, n_inner, heads, groups = sizes
    rows = q.shape[0]
    slots = n_inner + 1
    mine = heads // n_dp
    dp, outer, inner = (lax.axis_index(name) for name in ("dp", "outer", "inner"))
    lower = lax.rem(outer + n_outer - 1, n_outer)
    upper = lax.rem(outer + 1, n_outer)

    def owner(slot):
        return {"outer": lower} if slot == n_inner else {"inner": lax.rem(inner + slot, n_inner)}

    def reader(slot):
        if slot == n_inner:
            return {"outer": upper}
        return {"inner": lax.rem(inner + n_inner - slot, n_inner)}

    def columns(head):
        return pl.ds(pl.multiple_of(head * HD, HD), HD)

    step_heads = [lax.rem(mine * (dp + 1) + k, heads) for k in range(heads)]

    local = [
        pltpu.make_async_copy(src, dst, local_sem.at[i])
        for i, (src, dst) in enumerate(
            ((k_hbm, kw.at[pl.ds(0, rows)]), (q_hbm, q), (v_hbm, vw.at[pl.ds(0, rows)]), (g_hbm, g))
        )
    ]
    for copy in local:
        copy.start()

    barrier = pltpu.get_barrier_semaphore()
    near = [{"inner": lax.rem(inner + i, n_inner)} for i in range(1, n_inner)]
    near += [{"dp": lax.rem(dp + i, n_dp)} for i in range(1, n_dp)]
    near += [{"outer": lower}, {"outer": upper}]
    for device in near:
        pl.semaphore_signal(barrier, inc=1, device_id=device, device_id_type=MESH)
    pl.semaphore_wait(barrier, len(near))

    def window(ref, slot, k):
        return ref.at[pl.ds(slot * rows, rows), columns(step_heads[k])]

    def arriving(src, dst, k, slot, which, send_sem, device, at):
        return pltpu.make_async_remote_copy(
            src_ref=src,
            dst_ref=window(dst, slot, k),
            send_sem=send_sem,
            recv_sem=kv_recv.at[at, slot - 1, which],
            device_id=device,
            device_id_type=MESH,
        )

    pairs = ((k_hbm, kw), (v_hbm, vw))
    arrivals = {}
    sent = []
    for k in range(heads):
        for slot in range(1, slots):
            direct = slot == n_inner or k < mine
            for which, (src, dst) in enumerate(pairs):
                block = src.at[:, columns(step_heads[k])] if direct else window(dst, slot, k)
                copy = arriving(
                    block, dst, k, slot, which, kv_send.at[k, slot - 1, which], reader(slot), k
                )
                if direct:
                    copy.start()
                    sent.append(copy)
                arrivals[k, slot, which] = copy

    def arrive(k):
        for slot in range(1, slots):
            for which, (_, dst) in enumerate(pairs):
                arrivals[k, slot, which].wait_recv()
                if slot == n_inner or k >= mine:
                    continue
                for d in range(1, n_dp):
                    copy = arriving(
                        window(dst, slot, k),
                        dst,
                        k,
                        slot,
                        which,
                        pass_send.at[d - 1, k, slot - 1, which],
                        {"dp": lax.rem(dp + d, n_dp)},
                        mine * (n_dp - d) + k,
                    )
                    copy.start()
                    sent.append(copy)

    shard = outer * n_inner + inner
    own_block = order[shard]
    bias = []
    for slot in range(1, slots):
        if slot == n_inner:
            place, block = n_inner, order[lower * n_inner + inner]
        else:
            place = lax.rem(inner + slot, n_inner)
            block = order[outer * n_inner + place]
        seen = (flags[place, shard] == 1) & (block < own_block)
        bias.append(jnp.where(seen, 0.0, HIDDEN).astype(jnp.float32))

    wide = groups * rows
    key_at = lax.broadcasted_iota(jnp.int32, (rows, wide), 0)
    query_at = lax.rem(lax.broadcasted_iota(jnp.int32, (rows, wide), 1), rows)
    causal = key_at <= query_at
    scale = 1.0 / math.sqrt(HD)
    to_exp2 = scale * math.log2(math.e)

    def nt(a, b):
        return lax.dot_general(a, b, (((1,), (1,)), ((), ())), preferred_element_type=jnp.float32)

    def nn(a, b):
        return jnp.dot(a, b, preferred_element_type=jnp.float32)

    grads = {}
    crossing = {}
    halves = []

    def crosses(k, slot):
        return slot < n_inner and k < heads - mine and k % mine < mine // 2


    def settle(k):
        total = acc[k]
        for slot in range(1, slots):
            if crosses(k, slot):
                continue
            grads[k, slot].wait_recv()
            total += grad_in[k, slot - 1].astype(jnp.float32)
        if k < heads - mine:
            half_out[k] = total.astype(jnp.bfloat16)
            copy = pltpu.make_async_remote_copy(
                src_ref=half_out.at[k],
                dst_ref=half_in.at[k],
                send_sem=half_send.at[k],
                recv_sem=half_recv.at[k],
                device_id={"dp": lax.rem(dp + 1 + k // mine, n_dp)},
                device_id_type=MESH,
            )
            copy.start()
            halves.append(copy)
        else:
            at = k - (heads - mine)
            for d in range(n_dp - 1):
                halves[d * mine + at].wait_recv()
                total += half_in[d * mine + at].astype(jnp.float32)
            kg_out[:, at * HD : (at + 1) * HD] = total[0]
            vg_out[:, at * HD : (at + 1) * HD] = total[1]

    def stacked(k):
        group_cols = [columns(n * heads + step_heads[k]) for n in range(groups)]
        q_all = jnp.concatenate([q[:, c] for c in group_cols], 0)
        g_all = jnp.concatenate([g[:, c] for c in group_cols], 0)
        return group_cols, q_all, g_all

    for copy in local:
        copy.wait()
    for k in range(heads):
        cols = columns(step_heads[k])
        _, q_all, g_all = stacked(k)
        own[k, 0] = jnp.where(causal, nt(kw[:rows, cols], q_all), HIDDEN)
        own[k, 1] = nt(vw[:rows, cols], g_all)
    for k in range(heads):
        cols = columns(step_heads[k])
        group_cols, q_all, g_all = stacked(k)
        arrive(k)
        keys = kw[:, cols]
        values = vw[:, cols]
        scores = nt(keys[rows:], q_all)
        weight_grads = jnp.concatenate([own[k, 1], nt(values[rows:], g_all)], 0)
        parts = [own[k, 0]] + [scores[c * rows : (c + 1) * rows] for c in range(slots - 1)]
        tops = [jnp.max(part, 0, keepdims=True) for part in parts]
        top = tops[0]
        for c in range(1, slots):
            top = jnp.maximum(top, tops[c] + bias[c - 1])
        exps = [
            jnp.exp2((part - (top if c == 0 else top - bias[c - 1])) * to_exp2)
            for c, part in enumerate(parts)
        ]
        weights = jnp.concatenate(exps, 0)
        soft = weights * (1.0 / jnp.sum(weights, 0, keepdims=True))
        delta = jnp.sum(soft * weight_grads, 0, keepdims=True)
        score_grads = (soft * (weight_grads - delta) * scale).astype(jnp.bfloat16)
        soft_low = soft.astype(jnp.bfloat16)
        key_part = nn(score_grads, q_all)
        value_part = nn(soft_low, g_all)
        acc[k, 0] = key_part[:rows]
        acc[k, 1] = value_part[:rows]
        for slot in range(1, slots):
            terms = [x[slot * rows : (slot + 1) * rows] for x in (key_part, value_part)]
            at = k - (heads - mine)
            if at >= 0 and slot < n_inner and at < mine // 2:
                for d in range(n_dp - 1):
                    crossing[d * mine + at, slot].wait_recv()
                    for which in range(2):
                        terms[which] += cross_in[d * mine + at, slot - 1, which].astype(jnp.float32)
            for which in range(2):
                grad_out[k, slot - 1, which] = terms[which].astype(jnp.bfloat16)
            if crosses(k, slot):
                copy = pltpu.make_async_remote_copy(
                    src_ref=grad_out.at[k, slot - 1],
                    dst_ref=cross_in.at[k, slot - 1],
                    send_sem=grad_send.at[k, slot - 1],
                    recv_sem=cross_recv.at[k, slot - 1],
                    device_id={"dp": lax.rem(dp + 1 + k // mine, n_dp)},
                    device_id_type=MESH,
                )
                crossing[k, slot] = copy
            else:
                copy = pltpu.make_async_remote_copy(
                    src_ref=grad_out.at[k, slot - 1],
                    dst_ref=grad_in.at[k, slot - 1],
                    send_sem=grad_send.at[k, slot - 1],
                    recv_sem=grad_recv.at[k, slot - 1],
                    device_id=owner(slot),
                    device_id_type=MESH,
                )
                grads[k, slot] = copy
            copy.start()
        query_part = nn(keys.T, score_grads)
        for n in range(groups):
            qg_out[:, group_cols[n]] = query_part[:, n * rows : (n + 1) * rows].T.astype(jnp.bfloat16)
        if k >= 2:
            settle(k - 2)
    for k in range(max(heads - 2, 0), heads):
        settle(k)
    for copy in sent + list(grads.values()) + list(crossing.values()) + halves:
        copy.wait_send()


def place(*refs):
    *arrays, sems = refs
    copies = [
        pltpu.make_async_copy(arrays[i], arrays[i + 3], sems.at[i]) for i in range(3)
    ]
    for copy in copies:
        copy.start()
    for copy in copies:
        copy.wait()


def solution(mesh):
    n_dp, n_outer, n_inner = (mesh.shape[name] for name in ("dp", "outer", "inner"))

    def body(queries, out_grad, key_rows, value_rows, block_order, block_flags):
        rows, width = queries.shape
        heads = key_rows.shape[1] // HD
        groups = width // (heads * HD)
        mine = heads // n_dp
        others = n_inner
        bf16, f32 = jnp.bfloat16, jnp.float32
        window = (n_inner + 1) * rows
        any_space = pl.BlockSpec(memory_space=pl.ANY)
        smem = pl.BlockSpec(memory_space=pltpu.SMEM)
        vmem = pl.BlockSpec(memory_space=pltpu.VMEM)
        dma = pltpu.SemaphoreType.DMA
        operands = [
            pltpu.with_memory_space_constraint(x, pltpu.HBM)
            for x in (queries, out_grad, key_rows, value_rows, block_order, block_flags.T)
        ]
        results = pl.pallas_call(
            functools.partial(kernel, (n_dp, n_outer, n_inner, heads, groups)),
            out_shape=(
                pltpu.VMEM((rows, width), bf16),
                pltpu.VMEM((rows, mine * HD), f32),
                pltpu.VMEM((rows, mine * HD), f32),
            ),
            in_specs=[any_space] * 4 + [smem] * 2,
            out_specs=(vmem, vmem, vmem),
            scratch_shapes=[
                pltpu.VMEM((rows, width), bf16),
                pltpu.VMEM((rows, width), bf16),
                pltpu.VMEM((window, heads * HD), bf16),
                pltpu.VMEM((window, heads * HD), bf16),
                pltpu.VMEM((heads, 2, rows, HD), f32),
                pltpu.VMEM((heads, others, 2, rows, HD), bf16),
                pltpu.VMEM((heads, others, 2, rows, HD), bf16),
                pltpu.VMEM((heads - mine, 2, rows, HD), bf16),
                pltpu.VMEM((heads - mine, 2, rows, HD), bf16),
                dma((4,)),
                dma((heads, others, 2)),
                dma((heads, others, 2)),
                dma((heads, others)),
                dma((heads, others)),
                dma((heads - mine,)),
                dma((heads - mine,)),
                pltpu.VMEM((heads - mine, others, 2, rows, HD), bf16),
                dma((heads - mine, others)),
                dma((n_dp - 1, mine, others, 2)),
                pltpu.VMEM((heads, 2, rows, groups * rows), f32),
            ],
            compiler_params=pltpu.CompilerParams(
                collective_id=0, has_side_effects=True, vmem_limit_bytes=40 * 1024 * 1024
            ),
        )(*operands)
        return pl.pallas_call(
            place,
            out_shape=tuple(pltpu.HBM(x.shape, x.dtype) for x in results),
            in_specs=[vmem] * 3,
            out_specs=(any_space,) * 3,
            scratch_shapes=[dma((3,))],
        )(*(pltpu.with_memory_space_constraint(x, pltpu.VMEM) for x in results))

    spread = P(("outer", "inner"), "dp")
    return jax.shard_map(
        body,
        mesh=mesh,
        in_specs=(spread, spread, P(("outer", "inner"), None), P(("outer", "inner"), None), P(), P()),
        out_specs=(spread, spread, spread),
        check_vma=False,
    )
```
